256 devices in a mesh: layer: 16 (over x, y), doc: 16 (over z, core).
Axes of the slice: x: 4, y: 4, z: 8, core: 2. Of those that a mesh axis runs over, the one named last changes fastest.
Arguments:
- stored: float32 [32, 1280, 4096], P('layer', 'doc'), may hold values from -0.09 to 0.09
- pool: float32 [32, 512, 4096], P('layer', 'doc'), may hold values from -6 to 6
- basis_out: float32 [32, 64, 64], P('layer'), may hold values from -0.75 to 0.75
- basis_in: float32 [32, 64, 64], P('layer'), may hold values from -0.75 to 0.75
- eigen: float32 [32, 4096], P('layer'), may hold values from 0.02 to 2
- block_counts: int32 [16], P('doc'), may hold values from 48 to 80, as said below
- slot_doc: int32 [1280], P('doc'), may hold values from 0 to 1023, as said below
- query_ids: int32 [512], replicated, may hold values from 0 to 511
Outputs:
- scores: float32 [1024, 512], P('doc', 'layer')
The draws below stay inside these ranges and needn't reach their ends.
Inputs may be any that keep to these rules, and one draw needn't show every extreme that they name: Block b holds block_counts[b] documents; they sum to 1024, and the largest is exactly 80. `slot_doc`: the first block_counts[b] slots of block b name distinct documents, and over all blocks every document is named by exactly one such slot; the other slots name arbitrary documents.
All inputs are finite; a program needn't handle non-finite values.
Results may differ from the reference program's by a relative error of at most 0.0001.
Values sent between devices are 32-bit elements; how exact they have to be, the bound alone decides.
A program may use at most 128 MiB of HBM per device.

```python
import math
import jax
import jax.numpy as jnp
from jax import lax

R_OUT = 64
R_IN = 64
GRAD = 4096
LAYERS = 32
DOC_DEV = 64
CAP = 80
DOCS = 1024
SLOTS = 1280
QUERIES = 512
N_DOC = 16


def shared_counts(key):
    half = N_DOC // 2
    spread = CAP - DOC_DEV
    delta = jax.random.randint(jax.random.fold_in(key, 11), (half,), 0, spread + 1)
    delta = delta.at[0].set(spread)
    signed = jnp.concatenate([delta, -delta])
    order = jax.random.permutation(jax.random.fold_in(key, 12), N_DOC)
    return (DOC_DEV + signed)[order].astype(jnp.int32)


def draw_block_counts(key, part):
    counts = shared_counts(key)
    return counts


def draw_slot_doc(key, part):
    counts = shared_counts(key)
    key = jax.random.fold_in(key, 5)
    order = jax.random.permutation(jax.random.fold_in(key, 1), DOCS).astype(jnp.int32)
    starts = jnp.cumsum(counts) - counts
    places = jnp.arange(CAP, dtype=jnp.int32)
    position = starts[:, None] + places[None, :]
    valid = places[None, :] < counts[:, None]
    filler = jax.random.randint(jax.random.fold_in(key, 2), (N_DOC, CAP), 0, DOCS)
    picked = order[jnp.minimum(position, DOCS - 1)]
    return jnp.where(valid, picked, filler).reshape(N_DOC * CAP).astype(jnp.int32)


def set_ends(array, rng, smallest, high):
    longest = array.shape.index(max(array.shape))
    spots = []
    for shift in (0, 1):
        where = [jax.random.randint(jax.random.fold_in(rng, axis), (), 0, length) for axis, length in enumerate(array.shape)]
        where[longest] = (where[longest] + shift) % array.shape[longest]
        spots.append(tuple(where))
    return array.at[spots[0]].set(smallest).at[spots[1]].set(high)


def block_levels(own_key, shape, cuts, smallest, largest):
    factor_of, own = 1.0, jax.random.fold_in(own_key, 6)
    for dim, parts in cuts:
        heights = jnp.exp(jax.random.uniform(jax.random.fold_in(own, dim), (parts,), jnp.float32, smallest / len(cuts), largest / len(cuts)))
        factor_of = factor_of * jnp.repeat(heights, shape[dim] // parts).reshape([-1 if axis == dim else 1 for axis in range(len(shape))])
    return factor_of


def noise(key, dims, scale, limit, cuts=(), kind=jnp.bfloat16):
    values = scale * jax.random.normal(key, dims, jnp.float32)
    if cuts:
        values = values * block_levels(key, dims, cuts, -0.22, 0.18)
    return jnp.clip(values, -limit, limit).astype(kind)


def setup_inputs(seed: int = 0) -> dict:
    key_list = jax.random.split(jax.random.key(seed), 9)
    stored = noise(key_list[0], (LAYERS, SLOTS, GRAD), 0.015625, 0.09, ((0, 16), (1, 16)), jnp.float32)
    pool = noise(key_list[1], (LAYERS, QUERIES, GRAD), 1.0, 6.0, ((0, 16), (1, 16)), jnp.float32)
    basis_out = noise(key_list[2], (LAYERS, R_OUT, R_OUT), R_OUT ** -0.5, 0.75, ((0, 16),), jnp.float32)
    basis_in = noise(key_list[3], (LAYERS, R_IN, R_IN), R_IN ** -0.5, 0.75, ((0, 16),), jnp.float32)
    eigen = jnp.clip(jnp.exp(math.log(2.0) - 4.6051702 * jax.random.uniform(key_list[4], (LAYERS, GRAD), jnp.float32) ** block_levels(key_list[4], (LAYERS, GRAD), ((0, 16),), -0.2, 0.2)), 0.02, 2.0)
    block_counts = draw_block_counts(jax.random.fold_in(key_list[8], 71), 0)
    slot_doc = draw_slot_doc(jax.random.fold_in(key_list[8], 71), 0)
    query_ids = set_ends(jax.random.randint(key_list[7], (QUERIES,), 0, QUERIES), jax.random.fold_in(key_list[7], 1), 0, QUERIES - 1).astype(jnp.int32)
    return {"stored": stored, "pool": pool, "basis_out": basis_out, "basis_in": basis_in, "eigen": eigen, "block_counts": block_counts, "slot_doc": slot_doc, "query_ids": query_ids}


def condition(raw, out_basis, in_basis, values):
    count = raw.shape[0]
    grid = raw.reshape(count, R_OUT, R_IN)
    rotated = jnp.einsum("ba,nbc,cd->nad", out_basis, grid, in_basis, precision=lax.Precision.HIGHEST)
    rotated = rotated / (values.reshape(R_OUT, R_IN) + 0.05)
    back = jnp.einsum("ab,nbd,cd->nac", out_basis, rotated, in_basis, precision=lax.Precision.HIGHEST)
    return back.reshape(count, R_OUT * R_IN)


def reference(stored, pool, basis_out, basis_in, eigen, block_counts, slot_doc, query_ids):
    queries = pool[:, query_ids]

    def one_layer(index, total):
        conditioned = condition(queries[index], basis_out[index], basis_in[index], eigen[index])
        return total + jnp.dot(stored[index], conditioned.T, precision=lax.Precision.HIGHEST)

    total = lax.fori_loop(0, LAYERS, one_layer, jnp.zeros((SLOTS, QUERIES), jnp.float32))
    places = jnp.arange(CAP, dtype=jnp.int32)
    valid = (places[None, :] < block_counts[:, None]).reshape(SLOTS)
    total = jnp.where(valid[:, None], total, jnp.zeros_like(total))
    return jnp.zeros((DOCS, QUERIES), jnp.float32).at[slot_doc].add(total)
```

```python
import functools

import jax
import jax.numpy as jnp
from jax import lax
from jax.experimental import pallas as pl
from jax.experimental.pallas import tpu as pltpu
from jax.sharding import PartitionSpec as P

R = 64
GRAD = 4096
CAP = 80
ROWS = 32
LANES = 128
Q = 4
KC = GRAD // Q
MESH = pl.DeviceIdType.MESH
F32 = jnp.float32
BF16 = jnp.bfloat16


def mm(a, b):
    return lax.dot_general(a, b, (((1,), (0,)), ((), ())), preferred_element_type=F32)


def mm_nt(a, b):
    return lax.dot_general(a, b, (((1,), (1,)), ((), ())), preferred_element_type=F32)


def exact(a, b, trans_b=False):
    dims = (((1,), (1 if trans_b else 0,)), ((), ()))
    return lax.dot_general(a, b, dims, precision=lax.Precision.HIGHEST, preferred_element_type=F32)


def split(x, axis):
    hi = x.astype(BF16)
    lo = (x - hi.astype(F32)).astype(BF16)
    return jnp.concatenate([hi, lo], axis=axis)


def fold(o):
    half = o.shape[0] // 2
    top = o[:half, :LANES] + o[:half, LANES:]
    return top + (o[half:, :LANES] + o[half:, LANES:])


def onehot(shape, left, right):
    a = lax.broadcasted_iota(jnp.int32, shape, 0)
    b = lax.broadcasted_iota(jnp.int32, shape, 1)
    return left(a) == right(b)


def kernel(
    n_lay, n_doc,
    stored, pool, bo, bi, eig, counts, docs, qids,
    out,
    G, X, T, DT, W, KI, KO, Pm, Sel, ids, oh, rsrc, rin, dsrc, din,
    load_sem, own_send, sib_send, own_recv, sib_recv,
    ids_send, ids_recv, lay_send, lay_recv, doc_send, doc_recv,
):
    n_z = n_doc // 2
    total = n_z * Q
    lay = lax.axis_index("layer")
    doc = lax.axis_index("doc")
    z = doc // 2
    c = doc % 2
    sib = z * 2 + (1 - c)
    right = ((z + 1) % n_z) * 2 + c
    left = ((z + n_z - 1) % n_z) * 2 + c
    mine = pl.ds(pl.multiple_of(c * ROWS, ROWS), ROWS)

    def lay_peer(k):
        return ((lay + k) % n_lay, doc)

    def doc_peer(k):
        return (lay, (doc + k) % n_doc)

    barrier = pltpu.get_barrier_semaphore()

    @pl.loop(1, n_lay)
    def _(k):
        pl.semaphore_signal(barrier, inc=1, device_id=lay_peer(k), device_id_type=MESH)

    @pl.loop(1, n_doc)
    def _(k):
        pl.semaphore_signal(barrier, inc=1, device_id=doc_peer(k), device_id_type=MESH)

    loads = []
    for l in range(2):
        loads.append(pltpu.make_async_copy(stored.at[l], X.at[l, pl.ds(0, CAP)], load_sem.at[l]))
    own_loads = []
    for d in range(2):
        for q in range(Q):
            own_loads.append(pltpu.make_async_copy(
                pool.at[d, :, pl.ds(q * KC, KC)], G.at[d, 0, q, mine], load_sem.at[2 + d * Q + q]))
    for copy in loads + own_loads:
        copy.start()

    pl.semaphore_wait(barrier, n_lay + n_doc - 2)

    def to_next(d, s, q, src):
        return pltpu.make_async_remote_copy(
            src_ref=src, dst_ref=G.at[d, s + 1, q, mine],
            send_sem=own_send.at[d], recv_sem=own_recv.at[d, s + 1, q],
            device_id=(lay, right if d == 0 else left), device_id_type=MESH)

    def to_sib(d, s, q, src):
        return pltpu.make_async_remote_copy(
            src_ref=src, dst_ref=G.at[d, s, q, mine],
            send_sem=sib_send.at[d], recv_sem=sib_recv.at[d, s, q],
            device_id=(lay, sib), device_id_type=MESH)

    for q in range(Q):
        for d in range(2):
            to_next(d, 0, q, pool.at[d, :, pl.ds(q * KC, KC)]).start()
    for q in range(Q):
        for d in range(2):
            to_sib(d, 0, q, pool.at[d, :, pl.ds(q * KC, KC)]).start()

    def service(i):
        s = i // Q
        q = i % Q
        for d in range(2):
            block = G.at[d, s, q, mine]
            pltpu.make_async_remote_copy(
                src_ref=block, dst_ref=block, send_sem=own_send.at[d],
                recv_sem=own_recv.at[d, s, q],
                device_id=(lay, right), device_id_type=MESH).wait_recv()

            @pl.when(s < n_z - 1)
            def _():
                to_next(d, s, q, block).start()

            to_sib(d, s, q, block).start()

    lane = lax.broadcasted_iota(jnp.int32, (8, LANES), 1)
    ids[0, :, :] = jnp.zeros((8, LANES), F32)
    ids[0, 0:1, 0:CAP] = docs[...].astype(F32)
    ids[0, :, :] = jnp.where(lane < counts[0], ids[0, :, :], -1.0)

    @pl.loop(1, n_doc)
    def _(k):
        pltpu.make_async_remote_copy(
            src_ref=ids.at[0], dst_ref=ids.at[k], send_sem=ids_send.at[0],
            recv_sem=ids_recv.at[k], device_id=doc_peer(k), device_id_type=MESH).start()

    n_pool = ROWS * n_doc
    n_query = ROWS * n_lay
    X[:, CAP:, :] = jnp.zeros((2, LANES - CAP, GRAD), F32)
    Pm[...] = jnp.zeros((n_pool, LANES), F32)
    qcol = jnp.broadcast_to(qids[...].astype(F32), (LANES, n_query)).T
    for t in range(n_pool // LANES):
        at = lax.broadcasted_iota(jnp.int32, (n_query, LANES), 1) + t * LANES
        Sel[:, t * LANES:(t + 1) * LANES] = jnp.where(qcol == at.astype(F32), 1.0, 0.0).astype(BF16)

    inner = jnp.where(onehot((4 * R, R), lambda a: a % R, lambda b: b), 1.0, 0.0)
    inner_mask = onehot((4 * R, 4 * R), lambda a: a // R, lambda b: b // R)
    outer = jnp.where(onehot((8 * R, R), lambda a: a // 8, lambda b: b), 1.0, 0.0)
    outer_mask = onehot((8 * R, 8 * R), lambda a: a % 8, lambda b: b % 8)

    at_chunk = Q
    for l in range(2):
        for index, trans in ((0, True), (1, False)):
            big = exact(exact(inner, bi[l], trans), inner, True)
            KI[index] = split(jnp.where(inner_mask, big, 0.0), 0)
            big = exact(exact(outer, bo[l], trans), outer, True)
            KO[index] = split(jnp.where(outer_mask, big, 0.0), 0)

        @pl.loop(0, GRAD // LANES)
        def _(t):
            row = 1.0 / (eig[l:l + 1, pl.ds(pl.multiple_of(t * LANES, LANES), LANES)] + 0.05)
            DT[pl.ds(t * 2, 2)] = jnp.broadcast_to(row, (LANES, LANES)).T.reshape(2, R, LANES)

        loads[l].wait()

        @pl.loop(0, 16)
        def _(t):
            x = X[l, :, pl.ds(pl.multiple_of(t * 256, 256), 256)]
            y = fold(mm_nt(KI[0], split(x, 0)))
            T[pl.ds(t * 4, 4)] = y.reshape(4, R, LANES)

        service(at_chunk)
        at_chunk += 1

        @pl.loop(0, 4)
        def _(g2):
            for half in range(2):
                group = pl.ds(pl.multiple_of(g2 * 16 + half * 8, 8), 8)
                y = T[:, group, :].reshape(8 * R, LANES)
                y = fold(mm(KO[0], split(y, 1))) * DT[:, group, :].reshape(8 * R, LANES)
                y = fold(mm(KO[1], split(y, 1)))
                T[:, group, :] = y.reshape(R, 8, LANES)
            service(at_chunk + g2)

        at_chunk += 4

        @pl.loop(0, 16)
        def _(t):
            y = T[pl.ds(t * 4, 4)].reshape(256, LANES)
            y = fold(mm(KI[1], split(y, 1)))
            W[l, pl.ds(pl.multiple_of(t * 256, 256), 256), :] = split(y, 1)

        service(at_chunk)
        at_chunk += 1

    for copy in own_loads:
        copy.wait()

    first = (doc * 64).astype(F32)
    at_doc = lax.broadcasted_iota(jnp.int32, (64, LANES), 0).astype(F32) + first

    @pl.loop(0, n_doc)
    def _(k):
        @pl.when(k > 0)
        def _():
            pltpu.make_async_remote_copy(
                src_ref=ids.at[0], dst_ref=ids.at[k], send_sem=ids_send.at[0],
                recv_sem=ids_recv.at[k], device_id=doc_peer(k), device_id_type=MESH).wait_recv()
        row = jnp.broadcast_to(ids[k, 0:1, :], (64, LANES))
        oh[k] = jnp.where(row == at_doc, 1.0, 0.0).astype(BF16)

    def compute(i):
        s = i // Q
        q = i % Q
        for d in range(2):
            block = G.at[d, s, q, pl.ds(pl.multiple_of((1 - c) * ROWS, ROWS), ROWS)]
            pltpu.make_async_remote_copy(
                src_ref=block, dst_ref=block, send_sem=sib_send.at[d],
                recv_sem=sib_recv.at[d, s, q],
                device_id=(lay, sib), device_id_type=MESH).wait_recv()
            where = (z + n_z - s) % n_z if d == 0 else (z + s) % n_z
            rows = pl.ds(pl.multiple_of(where * 64, 64), 64)
            w = W[d, pl.ds(pl.multiple_of(q * KC, KC), KC), :]
            Pm[rows, :] += fold(mm(split(G[d, s, q], 0), w))

    begin = at_chunk

    @pl.loop(begin, total)
    def _(i):
        service(i)
        compute(2 * (i - begin))
        compute(2 * (i - begin) + 1)

    @pl.loop(2 * (total - begin), total)
    def _(i):
        compute(i)

    picked = mm(Sel[...], split(Pm[...], 1))
    rsrc[...] = (picked[:, :LANES] + picked[:, LANES:]).reshape(n_lay, ROWS, LANES)

    def lay_copy(k):
        return pltpu.make_async_remote_copy(
            src_ref=rsrc.at[(lay + k) % n_lay], dst_ref=rin.at[k], send_sem=lay_send.at[0],
            recv_sem=lay_recv.at[k], device_id=lay_peer(k), device_id_type=MESH)

    @pl.loop(1, n_lay)
    def _(k):
        lay_copy(k).start()

    def drain(ref, sem):
        pltpu.make_async_remote_copy(
            src_ref=ref, dst_ref=ref, send_sem=sem, recv_sem=own_recv.at[0, 0, 0],
            device_id=(lay, sib), device_id_type=MESH).wait_send()

    for d in range(2):
        drain(G.at[d, pl.ds(0, n_z - 1), :, pl.ds(0, ROWS)], own_send.at[d])
        drain(G.at[d, :, :, pl.ds(0, ROWS)], sib_send.at[d])
    drain(ids.at[pl.ds(1, n_doc - 1)], ids_send.at[0])

    def add(k, acc):
        lay_copy(k).wait_recv()
        return acc + rin[k]

    dsrc[...] = lax.fori_loop(1, n_lay, add, rsrc[lay])

    def doc_copy(k):
        return pltpu.make_async_remote_copy(
            src_ref=dsrc, dst_ref=din.at[k], send_sem=doc_send.at[0],
            recv_sem=doc_recv.at[k], device_id=doc_peer(k), device_id_type=MESH)

    @pl.loop(1, n_doc)
    def _(k):
        doc_copy(k).start()

    drain(rsrc.at[pl.ds(0, n_lay - 1)], lay_send.at[0])

    def place(k, x, acc):
        hi = x.astype(BF16)
        rest = x - hi.astype(F32)
        mid = rest.astype(BF16)
        lo = (rest - mid.astype(F32)).astype(BF16)
        return acc + (mm_nt(oh[k], hi) + (mm_nt(oh[k], mid) + mm_nt(oh[k], lo)))

    def collect(k, acc):
        doc_copy(k).wait_recv()
        return place(k, din[k], acc)

    out[...] = lax.fori_loop(1, n_doc, collect, place(0, dsrc[...], jnp.zeros((64, ROWS), F32)))
    drain(din.at[pl.ds(1, n_doc - 1)], doc_send.at[0])


def on_device(n_lay, n_doc, stored, pool, basis_out, basis_in, eigen, block_counts, slot_doc, query_ids):
    n_z = n_doc // 2
    n_pool = ROWS * n_doc
    n_query = ROWS * n_lay
    vmem = pl.BlockSpec(memory_space=pltpu.VMEM)
    anywhere = pl.BlockSpec(memory_space=pl.ANY)
    dma = pltpu.SemaphoreType.DMA
    return pl.pallas_call(
        functools.partial(kernel, n_lay, n_doc),
        out_shape=jax.ShapeDtypeStruct((64, ROWS), F32),
        in_specs=[anywhere, anywhere, vmem, vmem, vmem,
                  pl.BlockSpec(memory_space=pltpu.SMEM), vmem, vmem],
        out_specs=vmem,
        scratch_shapes=[
            pltpu.VMEM((2, n_z, Q, 64, KC), F32),
            pltpu.VMEM((2, LANES, GRAD), F32),
            pltpu.VMEM((R, R, LANES), F32),
            pltpu.VMEM((R, R, LANES), F32),
            pltpu.VMEM((2, GRAD, 2 * LANES), BF16),
            pltpu.VMEM((2, 8 * R, 4 * R), BF16),
            pltpu.VMEM((2, 16 * R, 8 * R), BF16),
            pltpu.VMEM((n_pool, LANES), F32),
            pltpu.VMEM((n_query, n_pool), BF16),
            pltpu.VMEM((n_doc, 8, LANES), F32),
            pltpu.VMEM((n_doc, 64, LANES), BF16),
            pltpu.VMEM((n_lay, ROWS, LANES), F32),
            pltpu.VMEM((n_lay, ROWS, LANES), F32),
            pltpu.VMEM((ROWS, LANES), F32),
            pltpu.VMEM((n_doc, ROWS, LANES), F32),
            dma((2 + 2 * Q,)),
            dma((2,)),
            dma((2,)),
            dma((2, n_z, Q)),
            dma((2, n_z, Q)),
            dma((1,)),
            dma((n_doc,)),
            dma((1,)),
            dma((n_lay,)),
            dma((1,)),
            dma((n_doc,)),
        ],
        compiler_params=pltpu.CompilerParams(
            collective_id=0, has_side_effects=True, vmem_limit_bytes=56 * 1024 * 1024
        ),
        cost_estimate=pl.CostEstimate(flops=40_000_000_000, bytes_accessed=8_000_000, transcendentals=0),
    )(stored, pool, basis_out, basis_in, eigen, block_counts,
      slot_doc.reshape(1, CAP), query_ids.reshape(1, n_query))


def solution(mesh):
    return jax.shard_map(
        functools.partial(on_device, mesh.shape["layer"], mesh.shape["doc"]),
        mesh=mesh,
        in_specs=(
            P("layer", "doc", None),
            P("layer", "doc", None),
            P("layer", None, None),
            P("layer", None, None),
            P("layer", None),
            P("doc"),
            P("doc"),
            P(),
        ),
        out_specs=P("doc", "layer"),
        check_vma=False,
    )
```

```python
import functools

import jax
import jax.numpy as jnp
from jax import lax
from jax.experimental import pallas as pl
from jax.experimental.pallas import tpu as pltpu
from jax.sharding import PartitionSpec as P

R = 64
GRAD = 4096
CAP = 80
ROWS = 32
PACKED = 24
LANES = 128
Q = 4
KC = GRAD // Q
MESH = pl.DeviceIdType.MESH
F32 = jnp.float32
BF16 = jnp.bfloat16


def mm(a, b):
    return lax.dot_general(a, b, (((1,), (0,)), ((), ())), preferred_element_type=F32)


def mm_nt(a, b):
    return lax.dot_general(a, b, (((1,), (1,)), ((), ())), preferred_element_type=F32)


def exact(a, b, trans_b=False):
    dims = (((1,), (1 if trans_b else 0,)), ((), ()))
    return lax.dot_general(a, b, dims, precision=lax.Precision.HIGHEST, preferred_element_type=F32)


def split(x, axis):
    hi = x.astype(BF16)
    lo = (x - hi.astype(F32)).astype(BF16)
    return jnp.concatenate([hi, lo], axis=axis)


def fold(o):
    half = o.shape[0] // 2
    top = o[:half, :LANES] + o[:half, LANES:]
    return top + (o[half:, :LANES] + o[half:, LANES:])


def onehot(shape, left, right):
    a = lax.broadcasted_iota(jnp.int32, shape, 0)
    b = lax.broadcasted_iota(jnp.int32, shape, 1)
    return left(a) == right(b)


def kernel(
    n_lay, n_doc,
    stored, pool, bo_in, bi_in, eig_in, counts_in, docs_in, qids_in,
    out,
    bo, bi, eig, counts, docs, qids,
    G, X, T, DT, W, KI, KO, Pm, Sel, ids, oh, rsrc, rin, dsrc, din, placed, other,
    small_sem, load_sem, own_send, sib_send, own_recv, sib_recv,
    ids_send, ids_recv, lay_send, lay_recv, doc_send, doc_recv, pair_send, pair_recv,
):
    n_z = n_doc // 2
    total = n_z * Q
    lay = lax.axis_index("layer")
    doc = lax.axis_index("doc")
    z = doc // 2
    c = doc % 2
    sib = z * 2 + (1 - c)
    right = ((z + 1) % n_z) * 2 + c
    left = ((z + n_z - 1) % n_z) * 2 + c
    mine = pl.ds(pl.multiple_of(c * ROWS, ROWS), ROWS)

    def lay_peer(k):
        return ((lay + k) % n_lay, doc)

    def doc_peer(k):
        return (lay, ((z + k) % n_z) * 2 + c)

    barrier = pltpu.get_barrier_semaphore()

    @pl.loop(1, n_lay)
    def _(k):
        pl.semaphore_signal(barrier, inc=1, device_id=lay_peer(k), device_id_type=MESH)

    @pl.loop(1, n_z)
    def _(k):
        pl.semaphore_signal(barrier, inc=1, device_id=doc_peer(k), device_id_type=MESH)

    pl.semaphore_signal(barrier, inc=1, device_id=(lay, sib), device_id_type=MESH)

    smalls = [
        pltpu.make_async_copy(src, dst, small_sem.at[at])
        for at, (src, dst) in enumerate((
            (bo_in, bo), (bi_in, bi), (eig_in, eig), (counts_in, counts), (docs_in, docs), (qids_in, qids)))
    ]
    loads = []
    for l in range(2):
        loads.append(pltpu.make_async_copy(stored.at[l], X.at[l, pl.ds(0, CAP)], load_sem.at[l]))
    own_loads = []
    for d in range(2):
        for q in range(Q):
            own_loads.append(pltpu.make_async_copy(
                pool.at[d, :, pl.ds(q * KC, KC)], G.at[d, 0, q, mine], load_sem.at[2 + d * Q + q]))
    for copy in smalls + loads + own_loads:
        copy.start()

    pl.semaphore_wait(barrier, n_lay + n_z - 1)

    def to_next(d, s, q, src):
        return pltpu.make_async_remote_copy(
            src_ref=src, dst_ref=G.at[d, s + 1, q, mine],
            send_sem=own_send.at[d], recv_sem=own_recv.at[d, s + 1, q],
            device_id=(lay, right if d == 0 else left), device_id_type=MESH)

    def to_sib(d, s, q, src):
        return pltpu.make_async_remote_copy(
            src_ref=src, dst_ref=G.at[d, s, q, mine],
            send_sem=sib_send.at[d], recv_sem=sib_recv.at[d, s, q],
            device_id=(lay, sib), device_id_type=MESH)

    for q in range(Q):
        for d in range(2):
            to_next(d, 0, q, pool.at[d, :, pl.ds(q * KC, KC)]).start()
    for q in range(Q):
        for d in range(2):
            to_sib(d, 0, q, pool.at[d, :, pl.ds(q * KC, KC)]).start()

    def service(i):
        s = i // Q
        q = i % Q
        for d in range(2):
            block = G.at[d, s, q, mine]
            pltpu.make_async_remote_copy(
                src_ref=block, dst_ref=block, send_sem=own_send.at[d],
                recv_sem=own_recv.at[d, s, q],
                device_id=(lay, right), device_id_type=MESH).wait_recv()

            @pl.when(s < n_z - 1)
            def _():
                to_next(d, s, q, block).start()

            to_sib(d, s, q, block).start()

    for copy in smalls:
        copy.wait()

    lane = lax.broadcasted_iota(jnp.int32, (8, LANES), 1)
    ids[0, :, :] = jnp.zeros((8, LANES), F32)
    ids[0, 0:1, 0:CAP] = docs[...].astype(F32)
    ids[0, :, :] = jnp.where(lane < counts[0], ids[0, :, :], -1.0)

    @pl.loop(1, n_z)
    def _(k):
        pltpu.make_async_remote_copy(
            src_ref=ids.at[0], dst_ref=ids.at[k], send_sem=ids_send.at[0],
            recv_sem=ids_recv.at[k], device_id=doc_peer(k), device_id_type=MESH).start()

    n_pool = ROWS * n_doc
    n_query = ROWS * n_lay
    X[:, CAP:, :] = jnp.zeros((2, LANES - CAP, GRAD), F32)
    Pm[...] = jnp.zeros((n_pool, LANES), F32)
    qcol = jnp.broadcast_to(qids[...].astype(F32), (LANES, n_query)).T
    for t in range(n_pool // LANES):
        at = lax.broadcasted_iota(jnp.int32, (n_query, LANES), 1) + t * LANES
        Sel[:, t * LANES:(t + 1) * LANES] = jnp.where(qcol == at.astype(F32), 1.0, 0.0).astype(BF16)

    inner = jnp.where(onehot((4 * R, R), lambda a: a % R, lambda b: b), 1.0, 0.0)
    inner_mask = onehot((4 * R, 4 * R), lambda a: a // R, lambda b: b // R)
    outer = jnp.where(onehot((8 * R, R), lambda a: a // 8, lambda b: b), 1.0, 0.0)
    outer_mask = onehot((8 * R, 8 * R), lambda a: a % 8, lambda b: b % 8)

    at_chunk = Q
    for l in range(2):
        for index, trans in ((0, True), (1, False)):
            big = exact(exact(inner, bi[l], trans), inner, True)
            KI[index] = split(jnp.where(inner_mask, big, 0.0), 0)
            big = exact(exact(outer, bo[l], trans), outer, True)
            KO[index] = split(jnp.where(outer_mask, big, 0.0), 0)

        service(at_chunk)
        at_chunk += 1

        @pl.loop(0, GRAD // LANES)
        def _(t):
            row = 1.0 / (eig[l:l + 1, pl.ds(pl.multiple_of(t * LANES, LANES), LANES)] + 0.05)
            DT[pl.ds(t * 2, 2)] = jnp.broadcast_to(row, (LANES, LANES)).T.reshape(2, R, LANES)

        loads[l].wait()

        @pl.loop(0, 16)
        def _(t):
            x = X[l, :, pl.ds(pl.multiple_of(t * 256, 256), 256)]
            y = fold(mm_nt(KI[0], split(x, 0)))
            T[pl.ds(t * 4, 4)] = y.reshape(4, R, LANES)

        service(at_chunk)
        at_chunk += 1

        @pl.loop(0, 4)
        def _(g2):
            for half in range(2):
                group = pl.ds(pl.multiple_of(g2 * 16 + half * 8, 8), 8)
                y = T[:, group, :].reshape(8 * R, LANES)
                y = fold(mm(KO[0], split(y, 1))) * DT[:, group, :].reshape(8 * R, LANES)
                y = fold(mm(KO[1], split(y, 1)))
                T[:, group, :] = y.reshape(R, 8, LANES)
            service(at_chunk + g2)

        at_chunk += 4

        for part in range(2):
            @pl.loop(part * 8, part * 8 + 8)
            def _(t):
                y = T[pl.ds(t * 4, 4)].reshape(256, LANES)
                y = fold(mm(KI[1], split(y, 1)))
                W[l, pl.ds(pl.multiple_of(t * 256, 256), 256), :] = split(y, 1)

            service(at_chunk)
            at_chunk += 1

    for copy in own_loads:
        copy.wait()

    at_doc = (lax.broadcasted_iota(jnp.int32, (LANES, LANES), 0) + z * LANES).astype(F32)

    @pl.loop(0, n_z)
    def _(k):
        @pl.when(k > 0)
        def _():
            pltpu.make_async_remote_copy(
                src_ref=ids.at[0], dst_ref=ids.at[k], send_sem=ids_send.at[0],
                recv_sem=ids_recv.at[k], device_id=doc_peer(k), device_id_type=MESH).wait_recv()
        row = jnp.broadcast_to(ids[k, 0:1, :], (LANES, LANES))
        oh[k] = jnp.where(row == at_doc, 1.0, 0.0).astype(BF16)

    def compute(i):
        s = i // Q
        q = i % Q
        for d in range(2):
            block = G.at[d, s, q, pl.ds(pl.multiple_of((1 - c) * ROWS, ROWS), ROWS)]
            pltpu.make_async_remote_copy(
                src_ref=block, dst_ref=block, send_sem=sib_send.at[d],
                recv_sem=sib_recv.at[d, s, q],
                device_id=(lay, sib), device_id_type=MESH).wait_recv()
            where = (z + n_z - s) % n_z if d == 0 else (z + s) % n_z
            rows = pl.ds(pl.multiple_of(where * 64, 64), 64)
            w = W[d, pl.ds(pl.multiple_of(q * KC, KC), KC), :]
            Pm[rows, :] += fold(mm(split(G[d, s, q], 0), w))

    begin = at_chunk

    triple = min(total - begin, begin // 2)
    middle = begin + triple

    @pl.loop(begin, middle)
    def _(i):
        service(i)

        @pl.loop(0, 3)
        def _(j):
            compute(3 * (i - begin) + j)

    @pl.loop(middle, total)
    def _(i):
        service(i)
        compute(3 * triple + i - middle)

    @pl.loop(3 * triple + total - middle, total)
    def _(i):
        compute(i)

    picked = mm(Sel[...], split(Pm[...], 1))
    picked = (picked[:, :LANES] + picked[:, LANES:]).reshape(n_lay, ROWS, LANES)
    extra = picked[:, 24:].reshape(n_lay * 8, LANES)
    low = pltpu.roll(extra, 80, 1).reshape(n_lay, 8, LANES)
    high = pltpu.roll(extra, 40, 1).reshape(n_lay, 8, LANES)
    spare = lax.broadcasted_iota(jnp.int32, (n_lay, 8, LANES), 2) >= CAP
    rsrc[:, 0:8] = jnp.where(spare, low, picked[:, 0:8])
    rsrc[:, 8:16] = jnp.where(spare, high, picked[:, 8:16])
    rsrc[:, 16:24] = picked[:, 16:24]

    def lay_copy(k):
        return pltpu.make_async_remote_copy(
            src_ref=rsrc.at[(lay + k) % n_lay], dst_ref=rin.at[k], send_sem=lay_send.at[0],
            recv_sem=lay_recv.at[k], device_id=lay_peer(k), device_id_type=MESH)

    @pl.loop(1, n_lay)
    def _(k):
        lay_copy(k).start()

    def drain(ref, sem):
        pltpu.make_async_remote_copy(
            src_ref=ref, dst_ref=ref, send_sem=sem, recv_sem=own_recv.at[0, 0, 0],
            device_id=(lay, sib), device_id_type=MESH).wait_send()

    for d in range(2):
        drain(G.at[d, pl.ds(0, n_z - 1), :, pl.ds(0, ROWS)], own_send.at[d])
        drain(G.at[d, :, :, pl.ds(0, ROWS)], sib_send.at[d])
    drain(ids.at[pl.ds(1, n_z - 1)], ids_send.at[0])

    def add(k, acc):
        lay_copy(k).wait_recv()
        return acc + rin[k]

    dsrc[...] = lax.fori_loop(1, n_lay, add, rsrc[lay])

    def doc_copy(k):
        return pltpu.make_async_remote_copy(
            src_ref=dsrc, dst_ref=din.at[k], send_sem=doc_send.at[0],
            recv_sem=doc_recv.at[k], device_id=doc_peer(k), device_id_type=MESH)

    @pl.loop(1, n_z)
    def _(k):
        doc_copy(k).start()

    drain(rsrc.at[pl.ds(0, n_lay - 1)], lay_send.at[0])
    first = lax.broadcasted_iota(jnp.int32, (8, LANES), 1) < 40

    def place(k, x, acc):
        extra = jnp.where(first, pltpu.roll(x[0:8], 48, 1), pltpu.roll(x[8:16], 88, 1))
        x = jnp.concatenate([x, extra], axis=0)
        hi = x.astype(BF16)
        rest = x - hi.astype(F32)
        mid = rest.astype(BF16)
        lo = (rest - mid.astype(F32)).astype(BF16)
        three = jnp.concatenate([hi, mid, lo, jnp.zeros_like(lo)], axis=0)
        return acc + mm_nt(oh[k], three)

    def collect(k, acc):
        doc_copy(k).wait_recv()
        return place(k, din[k], acc)

    placed[...] = lax.fori_loop(1, n_z, collect, place(0, dsrc[...], jnp.zeros((LANES, LANES), F32)))
    pair = pltpu.make_async_remote_copy(
        src_ref=placed.at[pl.ds(pl.multiple_of((1 - c) * 64, 64), 64)], dst_ref=other,
        send_sem=pair_send, recv_sem=pair_recv, device_id=(lay, sib), device_id_type=MESH)
    pair.start()
    drain(din.at[pl.ds(1, n_z - 1)], doc_send.at[0])
    pair.wait()
    both = placed[pl.ds(pl.multiple_of(c * 64, 64), 64), :] + other[...]
    out[...] = both[:, 0:ROWS] + (both[:, ROWS:2 * ROWS] + both[:, 2 * ROWS:3 * ROWS])


def on_device(n_lay, n_doc, stored, pool, basis_out, basis_in, eigen, block_counts, slot_doc, query_ids):
    n_z = n_doc // 2
    n_pool = ROWS * n_doc
    n_query = ROWS * n_lay
    vmem = pl.BlockSpec(memory_space=pltpu.VMEM)
    anywhere = pl.BlockSpec(memory_space=pl.ANY)
    dma = pltpu.SemaphoreType.DMA
    return pl.pallas_call(
        functools.partial(kernel, n_lay, n_doc),
        out_shape=jax.ShapeDtypeStruct((64, ROWS), F32),
        in_specs=[anywhere] * 8,
        out_specs=vmem,
        scratch_shapes=[
            pltpu.VMEM((2, R, R), F32),
            pltpu.VMEM((2, R, R), F32),
            pltpu.VMEM((2, GRAD), F32),
            pltpu.SMEM((1,), jnp.int32),
            pltpu.VMEM((1, CAP), jnp.int32),
            pltpu.VMEM((1, n_query), jnp.int32),
            pltpu.VMEM((2, n_z, Q, 64, KC), F32),
            pltpu.VMEM((2, LANES, GRAD), F32),
            pltpu.VMEM((R, R, LANES), F32),
            pltpu.VMEM((R, R, LANES), F32),
            pltpu.VMEM((2, GRAD, 2 * LANES), BF16),
            pltpu.VMEM((2, 8 * R, 4 * R), BF16),
            pltpu.VMEM((2, 16 * R, 8 * R), BF16),
            pltpu.VMEM((n_pool, LANES), F32),
            pltpu.VMEM((n_query, n_pool), BF16),
            pltpu.VMEM((n_z, 8, LANES), F32),
            pltpu.VMEM((n_z, LANES, LANES), BF16),
            pltpu.VMEM((n_lay, PACKED, LANES), F32),
            pltpu.VMEM((n_lay, PACKED, LANES), F32),
            pltpu.VMEM((PACKED, LANES), F32),
            pltpu.VMEM((n_z, PACKED, LANES), F32),
            pltpu.VMEM((LANES, LANES), F32),
            pltpu.VMEM((64, LANES), F32),
            dma((6,)),
            dma((2 + 2 * Q,)),
            dma((2,)),
            dma((2,)),
            dma((2, n_z, Q)),
            dma((2, n_z, Q)),
            dma((1,)),
            dma((n_z,)),
            dma((1,)),
            dma((n_lay,)),
            dma((1,)),
            dma((n_z,)),
            dma(()),
            dma(()),
        ],
        compiler_params=pltpu.CompilerParams(
            collective_id=0, has_side_effects=True, vmem_limit_bytes=56 * 1024 * 1024
        ),
        cost_estimate=pl.CostEstimate(flops=40_000_000_000, bytes_accessed=8_000_000, transcendentals=0),
    )(stored, pool, basis_out, basis_in, eigen, block_counts,
      slot_doc.reshape(1, CAP), query_ids.reshape(1, n_query))


def solution(mesh):
    return jax.shard_map(
        functools.partial(on_device, mesh.shape["layer"], mesh.shape["doc"]),
        mesh=mesh,
        in_specs=(
            P("layer", "doc", None),
            P("layer", "doc", None),
            P("layer", None, None),
            P("layer", None, None),
            P("layer", None),
            P("doc"),
            P("doc"),
            P(),
        ),
        out_specs=P("doc", "layer"),
        check_vma=False,
    )
```

```python
import functools

import jax
import jax.numpy as jnp
from jax import lax
from jax.experimental import pallas as pl
from jax.experimental.pallas import tpu as pltpu
from jax.sharding import PartitionSpec as P

R = 64
GRAD = 4096
CAP = 80
ROWS = 32
PACKED = 24
LANES = 128
Q = 4
KC = GRAD // Q
MESH = pl.DeviceIdType.MESH
F32 = jnp.float32
BF16 = jnp.bfloat16


def mm(a, b):
    return lax.dot_general(a, b, (((1,), (0,)), ((), ())), preferred_element_type=F32)


def mm_nt(a, b):
    return lax.dot_general(a, b, (((1,), (1,)), ((), ())), preferred_element_type=F32)


def exact(a, b, trans_b=False):
    dims = (((1,), (1 if trans_b else 0,)), ((), ()))
    return lax.dot_general(a, b, dims, precision=lax.Precision.HIGHEST, preferred_element_type=F32)


def split(x, axis):
    hi = x.astype(BF16)
    lo = (x - hi.astype(F32)).astype(BF16)
    return jnp.concatenate([hi, lo], axis=axis)


def fold(o):
    half = o.shape[0] // 2
    top = o[:half, :LANES] + o[:half, LANES:]
    return top + (o[half:, :LANES] + o[half:, LANES:])


def onehot(shape, left, right):
    a = lax.broadcasted_iota(jnp.int32, shape, 0)
    b = lax.broadcasted_iota(jnp.int32, shape, 1)
    return left(a) == right(b)


def kernel(
    n_lay, n_doc,
    stored, pool, bo_in, bi_in, eig_in, counts_in, docs_in, qids_in,
    out,
    bo, bi, eig, counts, docs, qids,
    G, X, T, DT, W, KI, KO, Pm, Sel, ids, rsrc, rin, dsrc, din,
    small_sem, load_sem, own_send, sib_send, own_recv, sib_recv,
    lay_send, lay_recv, doc_send, doc_recv, relay,
):
    n_z = n_doc // 2
    total = n_z * Q
    lay = lax.axis_index("layer")
    doc = lax.axis_index("doc")
    z = doc // 2
    c = doc % 2
    sib = z * 2 + (1 - c)
    right = ((z + 1) % n_z) * 2 + c
    left = ((z + n_z - 1) % n_z) * 2 + c
    mine = pl.ds(pl.multiple_of(c * ROWS, ROWS), ROWS)

    def lay_peer(k):
        return ((lay + k) % n_lay, doc)

    def doc_peer(k):
        return (lay, (doc + k) % n_doc)

    barrier = pltpu.get_barrier_semaphore()

    n_y = 4 if n_lay == 16 else 2
    x, y = lay // n_y, lay % n_y
    along_x = [((lay + n_y) % n_lay, doc), ((lay + n_lay - n_y) % n_lay, doc)]
    along_y = [(x * n_y + (y + 1) % n_y, doc), (x * n_y + (y + n_y - 1) % n_y, doc)]
    for peer in [(lay, right), (lay, left), (lay, sib)] + along_x + along_y:
        pl.semaphore_signal(barrier, inc=1, device_id=peer, device_id_type=MESH)

    smalls = [
        pltpu.make_async_copy(src, dst, small_sem.at[at])
        for at, (src, dst) in enumerate((
            (bo_in, bo), (bi_in, bi), (eig_in, eig), (counts_in, counts), (docs_in, docs), (qids_in, qids)))
    ]
    loads = []
    for l in range(2):
        loads.append(pltpu.make_async_copy(stored.at[l], X.at[l, pl.ds(0, CAP)], load_sem.at[l]))
    own_loads = []
    for d in range(2):
        for q in range(Q):
            own_loads.append(pltpu.make_async_copy(
                pool.at[d, :, pl.ds(q * KC, KC)], G.at[d, 0, q, mine], load_sem.at[2 + d * Q + q]))
    for copy in smalls + loads + own_loads:
        copy.start()

    pl.semaphore_wait(barrier, 7)

    def to_next(d, s, q, src):
        return pltpu.make_async_remote_copy(
            src_ref=src, dst_ref=G.at[d, s + 1, q, mine],
            send_sem=own_send.at[d], recv_sem=own_recv.at[d, s + 1, q],
            device_id=(lay, right if d == 0 else left), device_id_type=MESH)

    def to_sib(d, s, q, src):
        return pltpu.make_async_remote_copy(
            src_ref=src, dst_ref=G.at[d, s, q, mine],
            send_sem=sib_send.at[d], recv_sem=sib_recv.at[d, s, q],
            device_id=(lay, sib), device_id_type=MESH)

    for q in range(Q):
        for d in range(2):
            to_next(d, 0, q, pool.at[d, :, pl.ds(q * KC, KC)]).start()
    for q in range(Q):
        for d in range(2):
            to_sib(d, 0, q, pool.at[d, :, pl.ds(q * KC, KC)]).start()

    def service(i):
        s = i // Q
        q = i % Q
        for d in range(2):
            block = G.at[d, s, q, mine]
            pltpu.make_async_remote_copy(
                src_ref=block, dst_ref=block, send_sem=own_send.at[d],
                recv_sem=own_recv.at[d, s, q],
                device_id=(lay, right), device_id_type=MESH).wait_recv()

            @pl.when(s < n_z - 1)
            def _():
                to_next(d, s, q, block).start()

            to_sib(d, s, q, block).start()

    for copy in smalls:
        copy.wait()

    def tell(step, peers):
        for peer in peers:
            pl.semaphore_signal(relay.at[step], inc=1, device_id=peer, device_id_type=MESH)

    tell(0, along_x)
    lane = lax.broadcasted_iota(jnp.int32, (8, LANES), 1)
    ids[...] = jnp.zeros((8, LANES), F32)
    ids[0:1, 0:CAP] = docs[...].astype(F32)
    ids[...] = jnp.where(lane < counts[0], ids[...], -1.0)

    n_pool = ROWS * n_doc
    n_query = ROWS * n_lay
    X[:, CAP:, :] = jnp.zeros((2, LANES - CAP, GRAD), F32)
    Pm[...] = jnp.zeros((n_pool, LANES), F32)
    qcol = jnp.broadcast_to(qids[...].astype(F32), (LANES, n_query)).T
    for t in range(n_pool // LANES):
        at = lax.broadcasted_iota(jnp.int32, (n_query, LANES), 1) + t * LANES
        Sel[:, t * LANES:(t + 1) * LANES] = jnp.where(qcol == at.astype(F32), 1.0, 0.0).astype(BF16)

    inner = jnp.where(onehot((4 * R, R), lambda a: a % R, lambda b: b), 1.0, 0.0)
    inner_mask = onehot((4 * R, 4 * R), lambda a: a // R, lambda b: b // R)
    outer = jnp.where(onehot((8 * R, R), lambda a: a // 8, lambda b: b), 1.0, 0.0)
    outer_mask = onehot((8 * R, 8 * R), lambda a: a % 8, lambda b: b % 8)

    at_chunk = Q
    for l in range(2):
        pl.semaphore_wait(relay.at[l], 2)
        tell(l + 1, along_y)
        for index, trans in ((0, True), (1, False)):
            big = exact(exact(inner, bi[l], trans), inner, True)
            KI[index] = split(jnp.where(inner_mask, big, 0.0), 0)
            big = exact(exact(outer, bo[l], trans), outer, True)
            KO[index] = split(jnp.where(outer_mask, big, 0.0), 0)

        service(at_chunk)
        at_chunk += 1

        @pl.loop(0, GRAD // LANES)
        def _(t):
            row = 1.0 / (eig[l:l + 1, pl.ds(pl.multiple_of(t * LANES, LANES), LANES)] + 0.05)
            DT[pl.ds(t * 2, 2)] = jnp.broadcast_to(row, (LANES, LANES)).T.reshape(2, R, LANES)

        loads[l].wait()

        @pl.loop(0, 16)
        def _(t):
            x = X[l, :, pl.ds(pl.multiple_of(t * 256, 256), 256)]
            y = fold(mm_nt(KI[0], split(x, 0)))
            T[pl.ds(t * 4, 4)] = y.reshape(4, R, LANES)

        service(at_chunk)
        at_chunk += 1

        @pl.loop(0, 4)
        def _(g2):
            for half in range(2):
                group = pl.ds(pl.multiple_of(g2 * 16 + half * 8, 8), 8)
                y = T[:, group, :].reshape(8 * R, LANES)
                y = fold(mm(KO[0], split(y, 1))) * DT[:, group, :].reshape(8 * R, LANES)
                y = fold(mm(KO[1], split(y, 1)))
                T[:, group, :] = y.reshape(R, 8, LANES)
            service(at_chunk + g2)

        at_chunk += 4

        for part in range(2):
            @pl.loop(part * 8, part * 8 + 8)
            def _(t):
                y = T[pl.ds(t * 4, 4)].reshape(256, LANES)
                y = fold(mm(KI[1], split(y, 1)))
                W[l, pl.ds(pl.multiple_of(t * 256, 256), 256), :] = split(y, 1)

            service(at_chunk)
            at_chunk += 1

    for copy in own_loads:
        copy.wait()

    pl.semaphore_wait(relay.at[2], 2)

    def compute(i):
        s = i // Q
        q = i % Q
        for d in range(2):
            block = G.at[d, s, q, pl.ds(pl.multiple_of((1 - c) * ROWS, ROWS), ROWS)]
            pltpu.make_async_remote_copy(
                src_ref=block, dst_ref=block, send_sem=sib_send.at[d],
                recv_sem=sib_recv.at[d, s, q],
                device_id=(lay, sib), device_id_type=MESH).wait_recv()
            where = (z + n_z - s) % n_z if d == 0 else (z + s) % n_z
            rows = pl.ds(pl.multiple_of(where * 64, 64), 64)
            w = W[d, pl.ds(pl.multiple_of(q * KC, KC), KC), :]
            Pm[rows, :] += fold(mm(split(G[d, s, q], 0), w))

    begin = at_chunk

    triple = min(total - begin, begin // 2)
    middle = begin + triple

    @pl.loop(begin, middle)
    def _(i):
        service(i)

        @pl.loop(0, 3)
        def _(j):
            compute(3 * (i - begin) + j)

    @pl.loop(middle, total)
    def _(i):
        service(i)
        compute(3 * triple + i - middle)

    @pl.loop(3 * triple + total - middle, total)
    def _(i):
        compute(i)

    picked = mm(Sel[...], split(Pm[...], 1))
    picked = (picked[:, :LANES] + picked[:, LANES:]).reshape(n_lay, ROWS, LANES)
    extra = picked[:, 24:].reshape(n_lay * 8, LANES)
    low = pltpu.roll(extra, 80, 1).reshape(n_lay, 8, LANES)
    high = pltpu.roll(extra, 40, 1).reshape(n_lay, 8, LANES)
    spare = lax.broadcasted_iota(jnp.int32, (n_lay, 8, LANES), 2) >= CAP
    rsrc[:, 0:8] = jnp.where(spare, low, picked[:, 0:8])
    rsrc[:, 8:16] = jnp.where(spare, high, picked[:, 8:16])
    rsrc[:, 16:24] = picked[:, 16:24]

    def lay_copy(k):
        return pltpu.make_async_remote_copy(
            src_ref=rsrc.at[(lay + k) % n_lay], dst_ref=rin.at[k], send_sem=lay_send.at[0],
            recv_sem=lay_recv.at[k], device_id=lay_peer(k), device_id_type=MESH)

    @pl.loop(1, n_lay)
    def _(k):
        lay_copy(k).start()

    def drain(ref, sem):
        pltpu.make_async_remote_copy(
            src_ref=ref, dst_ref=ref, send_sem=sem, recv_sem=own_recv.at[0, 0, 0],
            device_id=(lay, sib), device_id_type=MESH).wait_send()

    for d in range(2):
        drain(G.at[d, pl.ds(0, n_z - 1), :, pl.ds(0, ROWS)], own_send.at[d])
        drain(G.at[d, :, :, pl.ds(0, ROWS)], sib_send.at[d])

    def add(k, acc):
        lay_copy(k).wait_recv()
        return acc + rin[k]

    dsrc[...] = lax.fori_loop(1, n_lay, add, rsrc[lay])
    row = lax.broadcasted_iota(jnp.int32, (8, LANES), 0)
    named = jnp.broadcast_to(ids[0:1, :], (8, LANES))
    named = jnp.where(row == 0, pltpu.roll(named, 80, 1), pltpu.roll(named, 40, 1))
    dsrc[16:24] = jnp.where((lane >= CAP) & (row < 2), named, dsrc[16:24])

    def doc_copy(k):
        return pltpu.make_async_remote_copy(
            src_ref=dsrc, dst_ref=din.at[k], send_sem=doc_send.at[0],
            recv_sem=doc_recv.at[k], device_id=doc_peer(k), device_id_type=MESH)

    @pl.loop(1, n_doc)
    def _(k):
        doc_copy(k).start()

    drain(rsrc.at[pl.ds(0, n_lay - 1)], lay_send.at[0])
    at_doc = (lax.broadcasted_iota(jnp.int32, (64, LANES), 0) + doc * 64).astype(F32)

    def place(x, acc):
        low = pltpu.roll(x, 48, 1)
        high = pltpu.roll(x, 88, 1)
        extra = jnp.where(lane < 40, low[0:8], high[8:16])
        named = jnp.where(lane[0:1] < 40, low[16:17], high[17:18])
        named = jnp.where(lane[0:1] < CAP, named, -1.0)
        hit = jnp.where(jnp.broadcast_to(named, (64, LANES)) == at_doc, 1.0, 0.0).astype(BF16)
        x = jnp.concatenate([x, extra], axis=0)
        hi = x.astype(BF16)
        rest = x - hi.astype(F32)
        mid = rest.astype(BF16)
        lo = (rest - mid.astype(F32)).astype(BF16)
        three = jnp.concatenate([hi, mid, lo, jnp.zeros_like(lo)], axis=0)
        return acc + mm_nt(hit, three)

    def collect(k, acc):
        doc_copy(k).wait_recv()
        return place(din[k], acc)

    both = lax.fori_loop(1, n_doc, collect, place(dsrc[...], jnp.zeros((64, LANES), F32)))
    out[...] = both[:, 0:ROWS] + (both[:, ROWS:2 * ROWS] + both[:, 2 * ROWS:3 * ROWS])
    drain(din.at[pl.ds(1, n_doc - 1)], doc_send.at[0])


def on_device(n_lay, n_doc, stored, pool, basis_out, basis_in, eigen, block_counts, slot_doc, query_ids):
    n_z = n_doc // 2
    n_pool = ROWS * n_doc
    n_query = ROWS * n_lay
    vmem = pl.BlockSpec(memory_space=pltpu.VMEM)
    anywhere = pl.BlockSpec(memory_space=pl.ANY)
    dma = pltpu.SemaphoreType.DMA
    return pl.pallas_call(
        functools.partial(kernel, n_lay, n_doc),
        out_shape=jax.ShapeDtypeStruct((64, ROWS), F32),
        in_specs=[anywhere] * 8,
        out_specs=vmem,
        scratch_shapes=[
            pltpu.VMEM((2, R, R), F32),
            pltpu.VMEM((2, R, R), F32),
            pltpu.VMEM((2, GRAD), F32),
            pltpu.SMEM((1,), jnp.int32),
            pltpu.VMEM((1, CAP), jnp.int32),
            pltpu.VMEM((1, n_query), jnp.int32),
            pltpu.VMEM((2, n_z, Q, 64, KC), F32),
            pltpu.VMEM((2, LANES, GRAD), F32),
            pltpu.VMEM((R, R, LANES), F32),
            pltpu.VMEM((R, R, LANES), F32),
            pltpu.VMEM((2, GRAD, 2 * LANES), BF16),
            pltpu.VMEM((2, 8 * R, 4 * R), BF16),
            pltpu.VMEM((2, 16 * R, 8 * R), BF16),
            pltpu.VMEM((n_pool, LANES), F32),
            pltpu.VMEM((n_query, n_pool), BF16),
            pltpu.VMEM((8, LANES), F32),
            pltpu.VMEM((n_lay, PACKED, LANES), F32),
            pltpu.VMEM((n_lay, PACKED, LANES), F32),
            pltpu.VMEM((PACKED, LANES), F32),
            pltpu.VMEM((n_doc, PACKED, LANES), F32),
            dma((6,)),
            dma((2 + 2 * Q,)),
            dma((2,)),
            dma((2,)),
            dma((2, n_z, Q)),
            dma((2, n_z, Q)),
            dma((1,)),
            dma((n_lay,)),
            dma((1,)),
            dma((n_doc,)),
            pltpu.SemaphoreType.REGULAR((3,)),
        ],
        compiler_params=pltpu.CompilerParams(
            collective_id=0, has_side_effects=True, vmem_limit_bytes=56 * 1024 * 1024
        ),
        cost_estimate=pl.CostEstimate(flops=40_000_000_000, bytes_accessed=8_000_000, transcendentals=0),
    )(stored, pool, basis_out, basis_in, eigen, block_counts,
      slot_doc.reshape(1, CAP), query_ids.reshape(1, n_query))


def solution(mesh):
    return jax.shard_map(
        functools.partial(on_device, mesh.shape["layer"], mesh.shape["doc"]),
        mesh=mesh,
        in_specs=(
            P("layer", "doc", None),
            P("layer", "doc", None),
            P("layer", None, None),
            P("layer", None, None),
            P("layer", None),
            P("doc"),
            P("doc"),
            P(),
        ),
        out_specs=P("doc", "layer"),
        check_vma=False,
    )
```

```python
import functools

import jax
import jax.numpy as jnp
from jax import lax
from jax.experimental import pallas as pl
from jax.experimental.pallas import tpu as pltpu
from jax.sharding import PartitionSpec as P

R = 64
GRAD = 4096
CAP = 80
ROWS = 32
PACKED = 24
LANES = 128
Q = 4
KC = GRAD // Q
MESH = pl.DeviceIdType.MESH
F32 = jnp.float32
BF16 = jnp.bfloat16


def mm(a, b):
    return lax.dot_general(a, b, (((1,), (0,)), ((), ())), preferred_element_type=F32)


def mm_nt(a, b):
    return lax.dot_general(a, b, (((1,), (1,)), ((), ())), preferred_element_type=F32)


def exact(a, b, trans_b=False):
    dims = (((1,), (1 if trans_b else 0,)), ((), ()))
    return lax.dot_general(a, b, dims, precision=lax.Precision.HIGHEST, preferred_element_type=F32)


def split(x, axis):
    hi = x.astype(BF16)
    lo = (x - hi.astype(F32)).astype(BF16)
    return jnp.concatenate([hi, lo], axis=axis)


def fold(o):
    half = o.shape[0] // 2
    top = o[:half, :LANES] + o[:half, LANES:]
    return top + (o[half:, :LANES] + o[half:, LANES:])


def onehot(shape, left, right):
    a = lax.broadcasted_iota(jnp.int32, shape, 0)
    b = lax.broadcasted_iota(jnp.int32, shape, 1)
    return left(a) == right(b)


def kernel(
    n_lay, n_doc,
    stored, pool, bo_in, bi_in, eig_in, counts_in, docs_in, qids_in,
    out,
    bo, bi, eig, counts, docs, qids,
    G, X, T, DT, W, KI, KO, Pm, Sel, ids, hit, rsrc, rin, dsrc, din, placed, other,
    small_sem, load_sem, own_send, sib_send, own_recv, sib_recv,
    ids_send, ids_recv, lay_send, lay_recv, doc_send, doc_recv, pair_send, pair_recv, relay,
):
    n_z = n_doc // 2
    total = n_z * Q
    lay = lax.axis_index("layer")
    doc = lax.axis_index("doc")
    z = doc // 2
    c = doc % 2
    sib = z * 2 + (1 - c)
    right = ((z + 1) % n_z) * 2 + c
    left = ((z + n_z - 1) % n_z) * 2 + c
    mine = pl.ds(pl.multiple_of(c * ROWS, ROWS), ROWS)

    n_y = 4 if n_lay == 16 else 2
    n_x = n_lay // n_y
    x, y = lay // n_y, lay % n_y

    def far(k, n):
        return min(k, n - k)

    lay_order = sorted(range(1, n_lay), key=lambda k: -far(k // n_y, n_x) - far(k % n_y, n_y))
    doc_order = sorted(range(1, n_z), key=lambda k: -far(k, n_z))

    def lay_at(k):
        return (x + k // n_y) % n_x * n_y + (y + k % n_y) % n_y

    def doc_peer(k):
        return (lay, ((z + k) % n_z) * 2 + c)

    barrier = pltpu.get_barrier_semaphore()

    along_x = [((lay + n_y) % n_lay, doc), ((lay + n_lay - n_y) % n_lay, doc)]
    along_y = [(x * n_y + (y + 1) % n_y, doc), (x * n_y + (y + n_y - 1) % n_y, doc)]
    for peer in [(lay, right), (lay, left), (lay, sib)] + along_x + along_y:
        pl.semaphore_signal(barrier, inc=1, device_id=peer, device_id_type=MESH)

    smalls = [
        pltpu.make_async_copy(src, dst, small_sem.at[at])
        for at, (src, dst) in enumerate((
            (bo_in, bo), (bi_in, bi), (eig_in, eig), (counts_in, counts), (docs_in, docs), (qids_in, qids)))
    ]
    loads = []
    for l in range(2):
        loads.append(pltpu.make_async_copy(stored.at[l], X.at[l, pl.ds(0, CAP)], load_sem.at[l]))
    own_loads = []
    for d in range(2):
        for q in range(Q):
            own_loads.append(pltpu.make_async_copy(
                pool.at[d, :, pl.ds(q * KC, KC)], G.at[d, 0, q, mine], load_sem.at[2 + d * Q + q]))
    for copy in smalls + loads + own_loads:
        copy.start()

    pl.semaphore_wait(barrier, 7)

    def to_next(d, s, q, src):
        return pltpu.make_async_remote_copy(
            src_ref=src, dst_ref=G.at[d, s + 1, q, mine],
            send_sem=own_send.at[d], recv_sem=own_recv.at[d, s + 1, q],
            device_id=(lay, right if d == 0 else left), device_id_type=MESH)

    def to_sib(d, s, q, src):
        return pltpu.make_async_remote_copy(
            src_ref=src, dst_ref=G.at[d, s, q, mine],
            send_sem=sib_send.at[d], recv_sem=sib_recv.at[d, s, q],
            device_id=(lay, sib), device_id_type=MESH)

    for q in range(Q):
        for d in range(2):
            to_next(d, 0, q, pool.at[d, :, pl.ds(q * KC, KC)]).start()
    for q in range(Q):
        for d in range(2):
            to_sib(d, 0, q, pool.at[d, :, pl.ds(q * KC, KC)]).start()

    def service(i):
        s = i // Q
        q = i % Q
        for d in range(2):
            block = G.at[d, s, q, mine]
            pltpu.make_async_remote_copy(
                src_ref=block, dst_ref=block, send_sem=own_send.at[d],
                recv_sem=own_recv.at[d, s, q],
                device_id=(lay, right), device_id_type=MESH).wait_recv()

            @pl.when(s < n_z - 1)
            def _():
                to_next(d, s, q, block).start()

            to_sib(d, s, q, block).start()

    for copy in smalls:
        copy.wait()

    def tell(step, peers):
        for peer in peers:
            pl.semaphore_signal(relay.at[step], inc=1, device_id=peer, device_id_type=MESH)

    tell(0, along_x)
    lane = lax.broadcasted_iota(jnp.int32, (8, LANES), 1)
    ids[0] = jnp.zeros((8, LANES), F32)
    ids[0, 0:1, 0:CAP] = docs[...].astype(F32)
    ids[0] = jnp.where(lane < counts[0], ids[0], -1.0)

    n_pool = ROWS * n_doc
    n_query = ROWS * n_lay
    X[:, CAP:, :] = jnp.zeros((2, LANES - CAP, GRAD), F32)
    Pm[...] = jnp.zeros((n_pool, LANES), F32)
    qcol = jnp.broadcast_to(qids[...].astype(F32), (LANES, n_query)).T
    for t in range(n_pool // LANES):
        at = lax.broadcasted_iota(jnp.int32, (n_query, LANES), 1) + t * LANES
        Sel[:, t * LANES:(t + 1) * LANES] = jnp.where(qcol == at.astype(F32), 1.0, 0.0).astype(BF16)

    inner = jnp.where(onehot((4 * R, R), lambda a: a % R, lambda b: b), 1.0, 0.0)
    inner_mask = onehot((4 * R, 4 * R), lambda a: a // R, lambda b: b // R)
    outer = jnp.where(onehot((8 * R, R), lambda a: a // 8, lambda b: b), 1.0, 0.0)
    outer_mask = onehot((8 * R, 8 * R), lambda a: a % 8, lambda b: b % 8)

    at_chunk = Q
    for l in range(2):
        pl.semaphore_wait(relay.at[l], 2)
        tell(l + 1, along_y)
        for index, trans in ((0, True), (1, False)):
            big = exact(exact(inner, bi[l], trans), inner, True)
            KI[index] = split(jnp.where(inner_mask, big, 0.0), 0)
            big = exact(exact(outer, bo[l], trans), outer, True)
            KO[index] = split(jnp.where(outer_mask, big, 0.0), 0)

        service(at_chunk)
        at_chunk += 1

        @pl.loop(0, GRAD // LANES)
        def _(t):
            row = 1.0 / (eig[l:l + 1, pl.ds(pl.multiple_of(t * LANES, LANES), LANES)] + 0.05)
            DT[pl.ds(t * 2, 2)] = jnp.broadcast_to(row, (LANES, LANES)).T.reshape(2, R, LANES)

        loads[l].wait()

        @pl.loop(0, 16)
        def _(t):
            x = X[l, :, pl.ds(pl.multiple_of(t * 256, 256), 256)]
            y = fold(mm_nt(KI[0], split(x, 0)))
            T[pl.ds(t * 4, 4)] = y.reshape(4, R, LANES)

        service(at_chunk)
        at_chunk += 1

        @pl.loop(0, 4)
        def _(g2):
            for half in range(2):
                group = pl.ds(pl.multiple_of(g2 * 16 + half * 8, 8), 8)
                y = T[:, group, :].reshape(8 * R, LANES)
                y = fold(mm(KO[0], split(y, 1))) * DT[:, group, :].reshape(8 * R, LANES)
                y = fold(mm(KO[1], split(y, 1)))
                T[:, group, :] = y.reshape(R, 8, LANES)
            service(at_chunk + g2)

        at_chunk += 4

        for part in range(2):
            @pl.loop(part * 8, part * 8 + 8)
            def _(t):
                y = T[pl.ds(t * 4, 4)].reshape(256, LANES)
                y = fold(mm(KI[1], split(y, 1)))
                W[l, pl.ds(pl.multiple_of(t * 256, 256), 256), :] = split(y, 1)

            service(at_chunk)
            at_chunk += 1

    for copy in own_loads:
        copy.wait()

    pl.semaphore_wait(relay.at[2], 2)

    def ids_copy(k):
        return pltpu.make_async_remote_copy(
            src_ref=ids.at[0], dst_ref=ids.at[k], send_sem=ids_send.at[0],
            recv_sem=ids_recv.at[k], device_id=doc_peer(k), device_id_type=MESH)

    for k in doc_order:
        ids_copy(k).start()

    def compute(i):
        s = i // Q
        q = i % Q
        for d in range(2):
            block = G.at[d, s, q, pl.ds(pl.multiple_of((1 - c) * ROWS, ROWS), ROWS)]
            pltpu.make_async_remote_copy(
                src_ref=block, dst_ref=block, send_sem=sib_send.at[d],
                recv_sem=sib_recv.at[d, s, q],
                device_id=(lay, sib), device_id_type=MESH).wait_recv()
            where = (z + n_z - s) % n_z if d == 0 else (z + s) % n_z
            rows = pl.ds(pl.multiple_of(where * 64, 64), 64)
            w = W[d, pl.ds(pl.multiple_of(q * KC, KC), KC), :]
            Pm[rows, :] += fold(mm(split(G[d, s, q], 0), w))

    begin = at_chunk

    triple = min(total - begin, begin // 2)
    middle = begin + triple

    half = begin + triple // 2

    def triples(low, high):
        @pl.loop(low, high)
        def _(i):
            service(i)

            @pl.loop(0, 3)
            def _(j):
                compute(3 * (i - begin) + j)

    triples(begin, half)

    for k in doc_order:
        ids_copy(k).wait_recv()

    at_doc = (lax.broadcasted_iota(jnp.int32, (LANES, LANES), 1) + z * LANES).astype(F32)
    spare = (lane >= CAP) & (lane < CAP + 40)

    @pl.loop(0, n_z)
    def _(k):
        named = jnp.broadcast_to(ids[k, 0:1, :], (8, LANES))
        for at, row in enumerate((
            named,
            jnp.where(spare, pltpu.roll(named, 80, 1), -1.0),
            jnp.where(spare, pltpu.roll(named, 40, 1), -1.0),
        )):
            column = jnp.broadcast_to(row[0:1], (LANES, LANES)).T
            hit[pl.ds(pl.multiple_of(k * LANES, LANES), LANES), at * LANES:(at + 1) * LANES] = (
                jnp.where(column == at_doc, 1.0, 0.0).astype(BF16))

    triples(half, middle)

    @pl.loop(middle, total)
    def _(i):
        service(i)
        compute(3 * triple + i - middle)

    @pl.loop(3 * triple + total - middle, total)
    def _(i):
        compute(i)

    picked = mm(Sel[...], split(Pm[...], 1))
    picked = (picked[:, :LANES] + picked[:, LANES:]).reshape(n_lay, ROWS, LANES)
    extra = picked[:, 24:].reshape(n_lay * 8, LANES)
    low = pltpu.roll(extra, 80, 1).reshape(n_lay, 8, LANES)
    high = pltpu.roll(extra, 40, 1).reshape(n_lay, 8, LANES)
    spare = lax.broadcasted_iota(jnp.int32, (n_lay, 8, LANES), 2) >= CAP
    rsrc[:, 0:8] = jnp.where(spare, low, picked[:, 0:8])
    rsrc[:, 8:16] = jnp.where(spare, high, picked[:, 8:16])
    rsrc[:, 16:24] = picked[:, 16:24]

    def lay_copy(k):
        peer = lay_at(k)
        return pltpu.make_async_remote_copy(
            src_ref=rsrc.at[peer], dst_ref=rin.at[k], send_sem=lay_send.at[0],
            recv_sem=lay_recv.at[k], device_id=(peer, doc), device_id_type=MESH)

    for k in lay_order:
        lay_copy(k).start()

    def drain(ref, sem):
        pltpu.make_async_remote_copy(
            src_ref=ref, dst_ref=ref, send_sem=sem, recv_sem=own_recv.at[0, 0, 0],
            device_id=(lay, sib), device_id_type=MESH).wait_send()

    for d in range(2):
        drain(G.at[d, pl.ds(0, n_z - 1), :, pl.ds(0, ROWS)], own_send.at[d])
        drain(G.at[d, :, :, pl.ds(0, ROWS)], sib_send.at[d])

    drain(ids.at[pl.ds(1, n_z - 1)], ids_send.at[0])

    acc = rsrc[lay]
    for k in lay_order[::-1]:
        lay_copy(k).wait_recv()
        acc = acc + rin[k]
    dsrc[...] = acc

    def doc_copy(k):
        return pltpu.make_async_remote_copy(
            src_ref=dsrc, dst_ref=din.at[k], send_sem=doc_send.at[0],
            recv_sem=doc_recv.at[k], device_id=doc_peer(k), device_id_type=MESH)

    for k in doc_order:
        doc_copy(k).start()

    drain(rsrc.at[pl.ds(0, n_lay - 1)], lay_send.at[0])
    for k in doc_order[::-1]:
        doc_copy(k).wait_recv()

    blocks = jnp.concatenate([dsrc[...]] + [din[k] for k in range(1, n_z)], axis=1)
    hi = blocks.astype(BF16).astype(F32)
    rest = blocks - hi
    mid = rest.astype(BF16).astype(F32)
    parts = jnp.concatenate([hi, mid, rest - mid, jnp.zeros((8, n_z * LANES), F32)], axis=0)
    parts = mm(parts.astype(BF16), hit[...])
    parts = parts[0:24] + (parts[24:48] + parts[48:72])
    last = parts[0:8, LANES:2 * LANES] + parts[8:16, 2 * LANES:]
    placed[...] = jnp.concatenate([parts[:, :LANES], last], axis=0)

    pair = pltpu.make_async_remote_copy(
        src_ref=placed, dst_ref=other, send_sem=pair_send, recv_sem=pair_recv,
        device_id=(lay, sib), device_id_type=MESH)
    pair.start()
    drain(din.at[pl.ds(1, n_z - 1)], doc_send.at[0])
    pair.wait()
    both = jnp.concatenate([placed[...] + other[...], jnp.zeros((LANES - ROWS, LANES), F32)], axis=0).T
    out[...] = jnp.where(c == 0, both[0:64], both[64:])[:, 0:ROWS]


def on_device(n_lay, n_doc, stored, pool, basis_out, basis_in, eigen, block_counts, slot_doc, query_ids):
    n_z = n_doc // 2
    n_pool = ROWS * n_doc
    n_query = ROWS * n_lay
    vmem = pl.BlockSpec(memory_space=pltpu.VMEM)
    anywhere = pl.BlockSpec(memory_space=pl.ANY)
    dma = pltpu.SemaphoreType.DMA
    return pl.pallas_call(
        functools.partial(kernel, n_lay, n_doc),
        out_shape=jax.ShapeDtypeStruct((64, ROWS), F32),
        in_specs=[anywhere] * 8,
        out_specs=vmem,
        scratch_shapes=[
            pltpu.VMEM((2, R, R), F32),
            pltpu.VMEM((2, R, R), F32),
            pltpu.VMEM((2, GRAD), F32),
            pltpu.SMEM((1,), jnp.int32),
            pltpu.VMEM((1, CAP), jnp.int32),
            pltpu.VMEM((1, n_query), jnp.int32),
            pltpu.VMEM((2, n_z, Q, 64, KC), F32),
            pltpu.VMEM((2, LANES, GRAD), F32),
            pltpu.VMEM((R, R, LANES), F32),
            pltpu.VMEM((R, R, LANES), F32),
            pltpu.VMEM((2, GRAD, 2 * LANES), BF16),
            pltpu.VMEM((2, 8 * R, 4 * R), BF16),
            pltpu.VMEM((2, 16 * R, 8 * R), BF16),
            pltpu.VMEM((n_pool, LANES), F32),
            pltpu.VMEM((n_query, n_pool), BF16),
            pltpu.VMEM((n_z, 8, LANES), F32),
            pltpu.VMEM((n_z * LANES, 3 * LANES), BF16),
            pltpu.VMEM((n_lay, PACKED, LANES), F32),
            pltpu.VMEM((n_lay, PACKED, LANES), F32),
            pltpu.VMEM((PACKED, LANES), F32),
            pltpu.VMEM((n_z, PACKED, LANES), F32),
            pltpu.VMEM((ROWS, LANES), F32),
            pltpu.VMEM((ROWS, LANES), F32),
            dma((6,)),
            dma((2 + 2 * Q,)),
            dma((2,)),
            dma((2,)),
            dma((2, n_z, Q)),
            dma((2, n_z, Q)),
            dma((1,)),
            dma((n_z,)),
            dma((1,)),
            dma((n_lay,)),
            dma((1,)),
            dma((n_z,)),
            dma(()),
            dma(()),
            pltpu.SemaphoreType.REGULAR((3,)),
        ],
        compiler_params=pltpu.CompilerParams(
            collective_id=0, has_side_effects=True, vmem_limit_bytes=56 * 1024 * 1024
        ),
        cost_estimate=pl.CostEstimate(flops=40_000_000_000, bytes_accessed=8_000_000, transcendentals=0),
    )(stored, pool, basis_out, basis_in, eigen, block_counts,
      slot_doc.reshape(1, CAP), query_ids.reshape(1, n_query))


def solution(mesh):
    return jax.shard_map(
        functools.partial(on_device, mesh.shape["layer"], mesh.shape["doc"]),
        mesh=mesh,
        in_specs=(
            P("layer", "doc", None),
            P("layer", "doc", None),
            P("layer", None, None),
            P("layer", None, None),
            P("layer", None),
            P("doc"),
            P("doc"),
            P(),
        ),
        out_specs=P("doc", "layer"),
        check_vma=False,
    )
```

```python
import functools

import jax
import jax.numpy as jnp
from jax import lax
from jax.experimental import pallas as pl
from jax.experimental.pallas import tpu as pltpu
from jax.sharding import PartitionSpec as P

R = 64
GRAD = 4096
CAP = 80
ROWS = 32
PACKED = 24
LANES = 128
Q = 4
KC = GRAD // Q
MESH = pl.DeviceIdType.MESH
F32 = jnp.float32
BF16 = jnp.bfloat16


def mm(a, b):
    return lax.dot_general(a, b, (((1,), (0,)), ((), ())), preferred_element_type=F32)


def mm_nt(a, b):
    return lax.dot_general(a, b, (((1,), (1,)), ((), ())), preferred_element_type=F32)


def exact(a, b, trans_b=False):
    dims = (((1,), (1 if trans_b else 0,)), ((), ()))
    return lax.dot_general(a, b, dims, precision=lax.Precision.HIGHEST, preferred_element_type=F32)


def split(x, axis):
    hi = x.astype(BF16)
    lo = (x - hi.astype(F32)).astype(BF16)
    return jnp.concatenate([hi, lo], axis=axis)


def fold(o):
    half = o.shape[0] // 2
    top = o[:half, :LANES] + o[:half, LANES:]
    return top + (o[half:, :LANES] + o[half:, LANES:])


def onehot(shape, left, right):
    a = lax.broadcasted_iota(jnp.int32, shape, 0)
    b = lax.broadcasted_iota(jnp.int32, shape, 1)
    return left(a) == right(b)


def kernel(
    n_lay, n_doc,
    stored, pool, bo_in, bi_in, eig_in, counts_in, docs_in, qids_in,
    out,
    bo, bi, eig, counts, docs, qids,
    G, X, T, DT, W, KI, KO, Pm, Sel, ids, hit, rsrc, rin, dsrc, din, placed, other,
    small_sem, load_sem, own_send, sib_send, own_recv, sib_recv,
    ids_send, ids_recv, lay_send, lay_recv, doc_send, doc_recv, pair_send, pair_recv, relay,
):
    n_z = n_doc // 2
    total = n_z * Q
    lay = lax.axis_index("layer")
    doc = lax.axis_index("doc")
    z = doc // 2
    c = doc % 2
    sib = z * 2 + (1 - c)
    right = ((z + 1) % n_z) * 2 + c
    left = ((z + n_z - 1) % n_z) * 2 + c
    mine = pl.ds(pl.multiple_of(c * ROWS, ROWS), ROWS)

    n_y = 4 if n_lay == 16 else 2
    n_x = n_lay // n_y
    x, y = lay // n_y, lay % n_y

    def far(k, n):
        return min(k, n - k)

    lay_order = sorted(range(1, n_lay), key=lambda k: -far(k // n_y, n_x) - far(k % n_y, n_y))
    doc_order = sorted(range(1, n_z), key=lambda k: -far(k, n_z))

    def lay_at(k):
        return (x + k // n_y) % n_x * n_y + (y + k % n_y) % n_y

    def doc_peer(k):
        return (lay, ((z + k) % n_z) * 2 + c)

    barrier = pltpu.get_barrier_semaphore()

    along_x = [((lay + n_y) % n_lay, doc), ((lay + n_lay - n_y) % n_lay, doc)]
    along_y = [(x * n_y + (y + 1) % n_y, doc), (x * n_y + (y + n_y - 1) % n_y, doc)]
    for peer in [(lay, right), (lay, left), (lay, sib)] + along_x + along_y:
        pl.semaphore_signal(barrier, inc=1, device_id=peer, device_id_type=MESH)

    smalls = [
        pltpu.make_async_copy(src, dst, small_sem.at[at])
        for at, (src, dst) in enumerate((
            (bo_in, bo), (bi_in, bi), (eig_in, eig), (counts_in, counts), (docs_in, docs), (qids_in, qids)))
    ]
    loads = []
    for l in range(2):
        loads.append(pltpu.make_async_copy(stored.at[l], X.at[l, pl.ds(0, CAP)], load_sem.at[l]))
    own_loads = []
    for d in range(2):
        for q in range(Q):
            own_loads.append(pltpu.make_async_copy(
                pool.at[d, :, pl.ds(q * KC, KC)], G.at[d, 0, q, mine], load_sem.at[2 + d * Q + q]))
    pl.semaphore_wait(barrier, 7)

    def to_next(d, s, q, src):
        return pltpu.make_async_remote_copy(
            src_ref=src, dst_ref=G.at[d, s + 1, q, mine],
            send_sem=own_send.at[d], recv_sem=own_recv.at[d, s + 1, q],
            device_id=(lay, right if d == 0 else left), device_id_type=MESH)

    def to_sib(d, s, q, src):
        return pltpu.make_async_remote_copy(
            src_ref=src, dst_ref=G.at[d, s, q, mine],
            send_sem=sib_send.at[d], recv_sem=sib_recv.at[d, s, q],
            device_id=(lay, sib), device_id_type=MESH)

    for q in range(Q):
        for d in range(2):
            to_next(d, 0, q, pool.at[d, :, pl.ds(q * KC, KC)]).start()
    for copy in smalls + loads:
        copy.start()
    for q in range(Q):
        for d in range(2):
            to_sib(d, 0, q, pool.at[d, :, pl.ds(q * KC, KC)]).start()

    for copy in own_loads:
        copy.start()

    def service(i):
        s = i // Q
        q = i % Q
        for d in range(2):
            block = G.at[d, s, q, mine]
            pltpu.make_async_remote_copy(
                src_ref=block, dst_ref=block, send_sem=own_send.at[d],
                recv_sem=own_recv.at[d, s, q],
                device_id=(lay, right), device_id_type=MESH).wait_recv()

            @pl.when(s < n_z - 1)
            def _():
                to_next(d, s, q, block).start()

            to_sib(d, s, q, block).start()

    for copy in smalls:
        copy.wait()

    def tell(step, peers):
        for peer in peers:
            pl.semaphore_signal(relay.at[step], inc=1, device_id=peer, device_id_type=MESH)

    tell(0, along_x)
    lane = lax.broadcasted_iota(jnp.int32, (8, LANES), 1)
    ids[0] = jnp.zeros((8, LANES), F32)
    ids[0, 0:1, 0:CAP] = docs[...].astype(F32)
    ids[0] = jnp.where(lane < jnp.broadcast_to(counts[...], (8, LANES)), ids[0], -1.0)

    n_pool = ROWS * n_doc
    n_query = ROWS * n_lay
    X[:, CAP:, :] = jnp.zeros((2, LANES - CAP, GRAD), F32)
    Pm[...] = jnp.zeros((n_pool, LANES), F32)
    qcol = jnp.broadcast_to(qids[...].astype(F32), (LANES, n_query)).T
    for t in range(n_pool // LANES):
        at = lax.broadcasted_iota(jnp.int32, (n_query, LANES), 1) + t * LANES
        Sel[:, t * LANES:(t + 1) * LANES] = jnp.where(qcol == at.astype(F32), 1.0, 0.0).astype(BF16)

    inner = jnp.where(onehot((4 * R, R), lambda a: a % R, lambda b: b), 1.0, 0.0)
    inner_mask = onehot((4 * R, 4 * R), lambda a: a // R, lambda b: b // R)
    outer = jnp.where(onehot((8 * R, R), lambda a: a // 8, lambda b: b), 1.0, 0.0)
    outer_mask = onehot((8 * R, 8 * R), lambda a: a % 8, lambda b: b % 8)

    at_chunk = Q
    for l in range(2):
        pl.semaphore_wait(relay.at[l], 2)
        tell(l + 1, along_y)
        for index, trans in ((0, True), (1, False)):
            big = exact(exact(inner, bi[l], trans), inner, True)
            KI[index] = split(jnp.where(inner_mask, big, 0.0), 0)
            big = exact(exact(outer, bo[l], trans), outer, True)
            KO[index] = split(jnp.where(outer_mask, big, 0.0), 0)

        service(at_chunk)
        at_chunk += 1

        @pl.loop(0, GRAD // LANES)
        def _(t):
            row = 1.0 / (eig[l:l + 1, pl.ds(pl.multiple_of(t * LANES, LANES), LANES)] + 0.05)
            DT[pl.ds(t * 2, 2)] = jnp.broadcast_to(row, (LANES, LANES)).T.reshape(2, R, LANES)

        loads[l].wait()

        @pl.loop(0, 16)
        def _(t):
            x = X[l, :, pl.ds(pl.multiple_of(t * 256, 256), 256)]
            y = fold(mm_nt(KI[0], split(x, 0)))
            T[pl.ds(t * 4, 4)] = y.reshape(4, R, LANES)

        service(at_chunk)
        at_chunk += 1

        @pl.loop(0, 4)
        def _(g2):
            for half in range(2):
                group = pl.ds(pl.multiple_of(g2 * 16 + half * 8, 8), 8)
                y = T[:, group, :].reshape(8 * R, LANES)
                y = fold(mm(KO[0], split(y, 1))) * DT[:, group, :].reshape(8 * R, LANES)
                y = fold(mm(KO[1], split(y, 1)))
                T[:, group, :] = y.reshape(R, 8, LANES)
            service(at_chunk + g2)

        at_chunk += 4

        for part in range(2):
            @pl.loop(part * 8, part * 8 + 8)
            def _(t):
                y = T[pl.ds(t * 4, 4)].reshape(256, LANES)
                y = fold(mm(KI[1], split(y, 1)))
                W[l, pl.ds(pl.multiple_of(t * 256, 256), 256), :] = split(y, 1)

            service(at_chunk)
            at_chunk += 1

    for copy in own_loads:
        copy.wait()

    pl.semaphore_wait(relay.at[2], 2)

    def ids_copy(k):
        return pltpu.make_async_remote_copy(
            src_ref=ids.at[0], dst_ref=ids.at[k], send_sem=ids_send.at[0],
            recv_sem=ids_recv.at[k], device_id=doc_peer(k), device_id_type=MESH)

    for k in doc_order:
        ids_copy(k).start()

    def compute(i):
        s = i // Q
        q = i % Q
        for d in range(2):
            block = G.at[d, s, q, pl.ds(pl.multiple_of((1 - c) * ROWS, ROWS), ROWS)]
            pltpu.make_async_remote_copy(
                src_ref=block, dst_ref=block, send_sem=sib_send.at[d],
                recv_sem=sib_recv.at[d, s, q],
                device_id=(lay, sib), device_id_type=MESH).wait_recv()
            where = (z + n_z - s) % n_z if d == 0 else (z + s) % n_z
            rows = pl.ds(pl.multiple_of(where * 64, 64), 64)
            w = W[d, pl.ds(pl.multiple_of(q * KC, KC), KC), :]
            Pm[rows, :] += fold(mm(split(G[d, s, q], 0), w))

    begin = at_chunk

    triple = min(total - begin, begin // 2)
    middle = begin + triple

    half = begin + triple // 2

    def triples(low, high):
        @pl.loop(low, high)
        def _(i):
            service(i)

            @pl.loop(0, 3)
            def _(j):
                compute(3 * (i - begin) + j)

    triples(begin, half)

    for k in doc_order:
        ids_copy(k).wait_recv()

    at_doc = (lax.broadcasted_iota(jnp.int32, (LANES, LANES), 1) + z * LANES).astype(F32)
    spare = (lane >= CAP) & (lane < CAP + 40)

    @pl.loop(0, n_z)
    def _(k):
        named = jnp.broadcast_to(ids[k, 0:1, :], (8, LANES))
        for at, row in enumerate((
            named,
            jnp.where(spare, pltpu.roll(named, 80, 1), -1.0),
            jnp.where(spare, pltpu.roll(named, 40, 1), -1.0),
        )):
            column = jnp.broadcast_to(row[0:1], (LANES, LANES)).T
            hit[pl.ds(pl.multiple_of(k * LANES, LANES), LANES), at * LANES:(at + 1) * LANES] = (
                jnp.where(column == at_doc, 1.0, 0.0).astype(BF16))

    triples(half, middle)

    @pl.loop(middle, total)
    def _(i):
        service(i)
        compute(3 * triple + i - middle)

    @pl.loop(3 * triple + total - middle, total)
    def _(i):
        compute(i)

    picked = mm(Sel[...], split(Pm[...], 1))
    picked = (picked[:, :LANES] + picked[:, LANES:]).reshape(n_lay, ROWS, LANES)
    extra = picked[:, 24:].reshape(n_lay * 8, LANES)
    low = pltpu.roll(extra, 80, 1).reshape(n_lay, 8, LANES)
    high = pltpu.roll(extra, 40, 1).reshape(n_lay, 8, LANES)
    spare = lax.broadcasted_iota(jnp.int32, (n_lay, 8, LANES), 2) >= CAP
    rsrc[:, 0:8] = jnp.where(spare, low, picked[:, 0:8])
    rsrc[:, 8:16] = jnp.where(spare, high, picked[:, 8:16])
    rsrc[:, 16:24] = picked[:, 16:24]

    def lay_copy(k):
        peer = lay_at(k)
        return pltpu.make_async_remote_copy(
            src_ref=rsrc.at[peer], dst_ref=rin.at[k], send_sem=lay_send.at[0],
            recv_sem=lay_recv.at[k], device_id=(peer, doc), device_id_type=MESH)

    for k in lay_order:
        lay_copy(k).start()

    def drain(ref, sem):
        pltpu.make_async_remote_copy(
            src_ref=ref, dst_ref=ref, send_sem=sem, recv_sem=own_recv.at[0, 0, 0],
            device_id=(lay, sib), device_id_type=MESH).wait_send()

    for d in range(2):
        drain(G.at[d, pl.ds(0, n_z - 1), :, pl.ds(0, ROWS)], own_send.at[d])
        drain(G.at[d, :, :, pl.ds(0, ROWS)], sib_send.at[d])

    drain(ids.at[pl.ds(1, n_z - 1)], ids_send.at[0])

    acc = rsrc[lay]
    for k in lay_order[::-1]:
        lay_copy(k).wait_recv()
        acc = acc + rin[k]
    dsrc[...] = acc

    def doc_copy(k):
        return pltpu.make_async_remote_copy(
            src_ref=dsrc, dst_ref=din.at[k], send_sem=doc_send.at[0],
            recv_sem=doc_recv.at[k], device_id=doc_peer(k), device_id_type=MESH)

    for k in doc_order:
        doc_copy(k).start()

    drain(rsrc.at[pl.ds(0, n_lay - 1)], lay_send.at[0])
    for k in doc_order[::-1]:
        doc_copy(k).wait_recv()

    blocks = jnp.concatenate([dsrc[...]] + [din[k] for k in range(1, n_z)], axis=1)
    hi = blocks.astype(BF16).astype(F32)
    rest = blocks - hi
    mid = rest.astype(BF16).astype(F32)
    parts = jnp.concatenate([hi, mid, rest - mid, jnp.zeros((8, n_z * LANES), F32)], axis=0)
    parts = mm(parts.astype(BF16), hit[...])
    parts = parts[0:24] + (parts[24:48] + parts[48:72])
    last = parts[0:8, LANES:2 * LANES] + parts[8:16, 2 * LANES:]
    placed[...] = jnp.concatenate([parts[:, :LANES], last], axis=0)

    pair = pltpu.make_async_remote_copy(
        src_ref=placed, dst_ref=other, send_sem=pair_send, recv_sem=pair_recv,
        device_id=(lay, sib), device_id_type=MESH)
    pair.start()
    drain(din.at[pl.ds(1, n_z - 1)], doc_send.at[0])
    pair.wait()
    out[0] = jnp.where(c == 0, placed[:, 0:64], placed[:, 64:])
    out[1] = jnp.where(c == 0, other[:, 0:64], other[:, 64:])


def on_device(n_lay, n_doc, stored, pool, basis_out, basis_in, eigen, block_counts, slot_doc, query_ids):
    n_z = n_doc // 2
    n_pool = ROWS * n_doc
    n_query = ROWS * n_lay
    vmem = pl.BlockSpec(memory_space=pltpu.VMEM)
    anywhere = pl.BlockSpec(memory_space=pl.ANY)
    dma = pltpu.SemaphoreType.DMA
    halves = pl.pallas_call(
        functools.partial(kernel, n_lay, n_doc),
        out_shape=jax.ShapeDtypeStruct((2, ROWS, 64), F32),
        in_specs=[anywhere] * 8,
        out_specs=vmem,
        scratch_shapes=[
            pltpu.VMEM((2, R, R), F32),
            pltpu.VMEM((2, R, R), F32),
            pltpu.VMEM((2, GRAD), F32),
            pltpu.VMEM((1, 1), jnp.int32),
            pltpu.VMEM((1, CAP), jnp.int32),
            pltpu.VMEM((1, n_query), jnp.int32),
            pltpu.VMEM((2, n_z, Q, 64, KC), F32),
            pltpu.VMEM((2, LANES, GRAD), F32),
            pltpu.VMEM((R, R, LANES), F32),
            pltpu.VMEM((R, R, LANES), F32),
            pltpu.VMEM((2, GRAD, 2 * LANES), BF16),
            pltpu.VMEM((2, 8 * R, 4 * R), BF16),
            pltpu.VMEM((2, 16 * R, 8 * R), BF16),
            pltpu.VMEM((n_pool, LANES), F32),
            pltpu.VMEM((n_query, n_pool), BF16),
            pltpu.VMEM((n_z, 8, LANES), F32),
            pltpu.VMEM((n_z * LANES, 3 * LANES), BF16),
            pltpu.VMEM((n_lay, PACKED, LANES), F32),
            pltpu.VMEM((n_lay, PACKED, LANES), F32),
            pltpu.VMEM((PACKED, LANES), F32),
            pltpu.VMEM((n_z, PACKED, LANES), F32),
            pltpu.VMEM((ROWS, LANES), F32),
            pltpu.VMEM((ROWS, LANES), F32),
            dma((6,)),
            dma((2 + 2 * Q,)),
            dma((2,)),
            dma((2,)),
            dma((2, n_z, Q)),
            dma((2, n_z, Q)),
            dma((1,)),
            dma((n_z,)),
            dma((1,)),
            dma((n_lay,)),
            dma((1,)),
            dma((n_z,)),
            dma(()),
            dma(()),
            pltpu.SemaphoreType.REGULAR((3,)),
        ],
        compiler_params=pltpu.CompilerParams(
            collective_id=0, has_side_effects=True, vmem_limit_bytes=56 * 1024 * 1024
        ),
        cost_estimate=pl.CostEstimate(flops=40_000_000_000, bytes_accessed=8_000_000, transcendentals=0),
    )(stored, pool, basis_out, basis_in, eigen, block_counts.reshape(1, 1),
      slot_doc.reshape(1, CAP), query_ids.reshape(1, n_query))
    return (halves[0] + halves[1]).T


def solution(mesh):
    return jax.shard_map(
        functools.partial(on_device, mesh.shape["layer"], mesh.shape["doc"]),
        mesh=mesh,
        in_specs=(
            P("layer", "doc", None),
            P("layer", "doc", None),
            P("layer", None, None),
            P("layer", None, None),
            P("layer", None),
            P("doc"),
            P("doc"),
            P(),
        ),
        out_specs=P("doc", "layer"),
        check_vma=False,
    )
```
